768 devices in a mesh: tile: 192 (over y_lo, z, x), col: 4 (over y_hi, core).
Axes of the slice: x: 4, y: 8 (y_hi: 2, y_lo: 4; y = y_hi * 4 + y_lo), z: 12, core: 2. Of those that a mesh axis runs over, the one named last changes fastest.
Arguments:
- tracer_old: float32 [192, 6, 128, 128], P('tile', None, 'col'), may hold values from -6 to 6
- u_face: float32 [192, 6, 128, 128], P('tile', None, 'col'), may hold values from -4 to 4
- v_face: float32 [192, 6, 128, 128], P('tile', None, 'col'), may hold values from -4 to 4
- depth_levels: int32 [192, 128, 128], P('tile', 'col'), may hold values from 0 to 6
- cotangent: float32 [192, 6, 128, 128], P('tile', None, 'col'), may hold values from -90 to 90
- surface_diag: float32 [192, 128, 128], P('tile', 'col'), may hold values from 0.2 to 8
- seam_flip: int32 [192], replicated, may hold values from 0 to 1
- step_index: int32 [1], replicated, may hold values from 0 to 23
Outputs:
- adj_tracer: float32 [192, 6, 128, 128], P('tile', None, 'col')
- adj_pressure: float32 [192, 128, 128], P('tile', 'col')
The draws below stay inside these ranges and needn't reach their ends.
All inputs are finite; a program needn't handle non-finite values.
Results may differ from the reference program's by a relative error of at most 0.0009.
Values sent between devices are 32-bit elements; how exact they have to be, the bound alone decides.
A program may use at most 32 MiB of HBM per device.

```python
import math
import jax
import jax.numpy as jnp
from jax import lax

K = 6
SY = 128
SX = 128
ITERS = 2
TILES = 192


def draw_cotangent(key, part):
    key = jax.random.fold_in(key, 7)
    base_key, row_key, col_key = jax.random.split(key, 3)
    full_shape = (TILES, K, SY, SX)
    tile_scale = 3.0 ** (jnp.arange(TILES, dtype=jnp.float32) / max(TILES - 1, 1))
    row_scale = jnp.exp(jax.random.uniform(row_key, (TILES, K, SY, 1), jnp.float32, 0.0, math.log(10.0)))
    col_scale = jnp.exp(jax.random.uniform(col_key, (TILES, 1, 1, SX), jnp.float32, 0.0, math.log(10.0)))
    values = jnp.clip(jax.random.normal(base_key, full_shape, jnp.float32), -6.0, 6.0)
    return 0.05 * values * tile_scale.reshape(TILES, 1, 1, 1) * row_scale * col_scale


def draw_surface_diag(key, part):
    key = jax.random.fold_in(key, 11)
    tile_frac = (jnp.arange(TILES, dtype=jnp.float32) / max(TILES - 1, 1)).reshape(TILES, 1, 1)
    cell_part = jax.random.uniform(key, (TILES, SY, SX), jnp.float32, 0.0, 1.0)
    exponent = 0.7 * tile_frac + 0.3 * cell_part
    return jnp.clip(0.2 * jnp.exp(math.log(40.0) * exponent), 0.2, 8.0)


def with_ends(drawn, stream_key, least, high):
    longest = drawn.shape.index(max(drawn.shape))
    spots = []
    for shift in (0, 1):
        where = [jax.random.randint(jax.random.fold_in(stream_key, axis), (), 0, length) for axis, length in enumerate(drawn.shape)]
        where[longest] = (where[longest] + shift) % drawn.shape[longest]
        spots.append(tuple(where))
    return drawn.at[spots[0]].set(least).at[spots[1]].set(high)


def block_scale(rng, extent, shards, least, largest):
    loudness, own = 1.0, jax.random.fold_in(rng, 6)
    for dim, parts in shards:
        draws = jnp.exp(jax.random.uniform(jax.random.fold_in(own, dim), (parts,), jnp.float32, least / len(shards), largest / len(shards)))
        loudness = loudness * jnp.repeat(draws, extent[dim] // parts).reshape([-1 if axis == dim else 1 for axis in range(len(extent))])
    return loudness


def scatter_about(stream_key, shape, scale, most, shards=(), kind=jnp.bfloat16):
    drawn = jax.random.normal(stream_key, shape, jnp.float32) * scale
    if len(shards) > 0:
        drawn = block_scale(stream_key, shape, shards, -0.22, 0.18) * drawn
    return jnp.clip(drawn, min=-most, max=most).astype(kind)


def setup_inputs(seed: int = 0) -> dict:
    keys = jax.random.split(jax.random.key(seed), 9)
    tracer_old = scatter_about(keys[0], (TILES, K, SY, SX), 1.0, 6.0, ((0, 192), (2, 4)), jnp.float32)
    u_face = scatter_about(keys[1], (TILES, K, SY, SX), 0.8, 4.0, ((0, 192), (2, 4)), jnp.float32)
    v_face = scatter_about(keys[2], (TILES, K, SY, SX), 0.8, 4.0, ((0, 192), (2, 4)), jnp.float32)
    depth_levels = with_ends(jax.random.randint(keys[3], (TILES, SY, SX), 0, K + 1), jax.random.fold_in(keys[3], 1), 0, K).astype(jnp.int32)
    cotangent = draw_cotangent(jax.random.fold_in(keys[8], 71), 0)
    surface_diag = draw_surface_diag(jax.random.fold_in(keys[8], 71), 0)
    seam_flip = with_ends(jax.random.randint(keys[6], (TILES,), 0, 2), jax.random.fold_in(keys[6], 1), 0, 1).astype(jnp.int32)
    step_index = jax.random.randint(keys[7], (1,), 0, 24).astype(jnp.int32)
    return {"tracer_old": tracer_old, "u_face": u_face, "v_face": v_face, "depth_levels": depth_levels, "cotangent": cotangent, "surface_diag": surface_diag, "seam_flip": seam_flip, "step_index": step_index}


flux_dt = 0.2
kappa_h = 0.4
kappa_base = 0.1
kappa_conv = 1.0
mix_dt = 0.3
relax_mean = 0.5
relax_swing = 0.8
day_steps = 24.0

def wet_levels(depth_float, level_count):
    level_ids = lax.broadcasted_iota(jnp.float32, (level_count,) + depth_float.shape, 0)
    return jnp.where(level_ids < depth_float[None], 1.0, 0.0).astype(jnp.float32)

def flux_divergence(tracer_ext, speed_ext, wet_ext, axis_num, cells):

    def window(values, offset):
        return lax.slice_in_dim(values, offset, offset + cells + 1, axis=axis_num)
    behind = window(tracer_ext, 0)
    center = window(tracer_ext, 1)
    front_cell = window(tracer_ext, 2)
    beyond = window(tracer_ext, 3)
    speeds = window(speed_ext, 1)
    open_face = window(wet_ext, 1) * window(wet_ext, 2)
    face_flux = open_face * (speeds * (7.0 * (center + front_cell) - (behind + beyond)) / 12.0 - kappa_h * (front_cell - center))
    return lax.slice_in_dim(face_flux, 1, cells + 1, axis=axis_num) - lax.slice_in_dim(face_flux, 0, cells, axis=axis_num)

def flux_adjoint(weight_ext, speed_ext, wet_ext, axis_num, cells):

    def window(values, offset, length):
        return lax.slice_in_dim(values, offset, offset + length, axis=axis_num)
    face_grad = flux_dt * (window(weight_ext, 1, cells + 3) - window(weight_ext, 0, cells + 3))
    open_face = window(wet_ext, 0, cells + 3) * window(wet_ext, 1, cells + 3)
    scaled = face_grad * open_face
    carried = window(speed_ext, 0, cells + 3) * scaled
    summed = -window(carried, 3, cells) / 12.0
    summed = summed + 7.0 * window(carried, 2, cells) / 12.0 + kappa_h * window(scaled, 2, cells)
    summed = summed + 7.0 * window(carried, 1, cells) / 12.0 - kappa_h * window(scaled, 1, cells)
    return summed - window(carried, 0, cells) / 12.0

def vertical_mix(column_state, wet_cells, relax_rate):
    upper_cells = column_state[:-1]
    lower_cells = column_state[1:]
    mix_coef = wet_cells[1:] * (kappa_base + kappa_conv * jax.nn.sigmoid(4.0 * (lower_cells - upper_cells)))
    face_flux = mix_coef * (upper_cells - lower_cells)
    boundary = jnp.zeros_like(column_state[:1])
    change = jnp.concatenate([face_flux, boundary]) - jnp.concatenate([boundary, face_flux])
    updated = column_state - mix_dt * change
    updated = jnp.concatenate([updated[:1] - relax_rate * column_state[:1], updated[1:]])
    return wet_cells * updated

def cotangent_after_mix(masked, masked_x, masked_y, u_x, v_y, wet_cells, wet_x, wet_y, weight_new, relax_rate):
    level_count, row_count, col_count = masked.shape
    change = flux_divergence(masked_x, u_x, wet_x, 2, col_count) + flux_divergence(masked_y, v_y, wet_y, 1, row_count)
    mixed = wet_cells * (masked - flux_dt * change)
    _, pullback = jax.vjp(lambda column_state: vertical_mix(column_state, wet_cells, relax_rate), mixed)
    return wet_cells * pullback(weight_new)[0]

def tracer_adjoint(weight_raw, raw_x, raw_y, u_x, v_y, wet_cells, wet_x, wet_y):
    level_count, row_count, col_count = weight_raw.shape
    summed = weight_raw + flux_adjoint(raw_x, u_x, wet_x, 2, col_count) + flux_adjoint(raw_y, v_y, wet_y, 1, row_count)
    return wet_cells * summed

def seam_neighbours(values, seam_flips, halo_width):
    col_count = values.shape[-1]
    east_cols = values[..., col_count - halo_width:]
    west_cols = values[..., :halo_width]
    shape_tail = (1,) * (values.ndim - 1)
    flip_west = jnp.roll(seam_flips, 1).reshape((-1,) + shape_tail) == 1
    flip_east = seam_flips.reshape((-1,) + shape_tail) == 1
    from_west = jnp.roll(east_cols, 1, axis=0)
    from_east = jnp.roll(west_cols, -1, axis=0)
    from_west = jnp.where(flip_west, jnp.flip(from_west, axis=-2), from_west)
    from_east = jnp.where(flip_east, jnp.flip(from_east, axis=-2), from_east)
    return (from_west, from_east)

def reference(tracer_old, u_face, v_face, depth_levels, cotangent, surface_diag, seam_flip, step_index):
    level_count = tracer_old.shape[1]
    depth_float = depth_levels.astype(jnp.float32)
    relax_rate = relax_mean * (1.0 + relax_swing * jnp.cos(2.0 * math.pi * step_index[0].astype(jnp.float32) / day_steps))
    old_west, old_east = seam_neighbours(tracer_old, seam_flip, 2)
    u_west, u_east = seam_neighbours(u_face, seam_flip, 2)
    depth_west, depth_east = seam_neighbours(depth_float, seam_flip, 2)

    def tile_fields(depth_tile, depth_w, depth_e, u_tile, u_w, u_e, v_tile):
        wet_cells = wet_levels(depth_tile, level_count)
        wet_x = wet_levels(jnp.concatenate([depth_w, depth_tile, depth_e], axis=-1), level_count)
        wet_y = wet_levels(jnp.pad(depth_tile, ((2, 2), (0, 0))), level_count)
        u_x = jnp.concatenate([u_w, u_tile, u_e], axis=-1)
        v_y = jnp.pad(v_tile, ((0, 0), (2, 2), (0, 0)))
        return (wet_cells, wet_x, wet_y, u_x, v_y)

    def first_pass(tile_items):
        old_tile, u_tile, v_tile, depth_tile, weight_tile, old_w, old_e, u_w, u_e, depth_w, depth_e = tile_items
        wet_cells, wet_x, wet_y, u_x, v_y = tile_fields(depth_tile, depth_w, depth_e, u_tile, u_w, u_e, v_tile)
        masked = old_tile * wet_cells
        masked_x = jnp.concatenate([old_w, old_tile, old_e], axis=-1) * wet_x
        masked_y = jnp.pad(masked, ((0, 0), (2, 2), (0, 0)))
        return cotangent_after_mix(masked, masked_x, masked_y, u_x, v_y, wet_cells, wet_x, wet_y, weight_tile, relax_rate)
    weight_raw = lax.map(first_pass, (tracer_old, u_face, v_face, depth_float, cotangent, old_west, old_east, u_west, u_east, depth_west, depth_east))
    raw_west, raw_east = seam_neighbours(weight_raw, seam_flip, 2)

    def second_pass(tile_items):
        raw_tile, u_tile, v_tile, depth_tile, raw_w, raw_e, u_w, u_e, depth_w, depth_e = tile_items
        wet_cells, wet_x, wet_y, u_x, v_y = tile_fields(depth_tile, depth_w, depth_e, u_tile, u_w, u_e, v_tile)
        raw_x = jnp.concatenate([raw_w, raw_tile, raw_e], axis=-1)
        raw_y = jnp.pad(raw_tile, ((0, 0), (2, 2), (0, 0)))
        return tracer_adjoint(raw_tile, raw_x, raw_y, u_x, v_y, wet_cells, wet_x, wet_y)
    adj_tracer = lax.map(second_pass, (weight_raw, u_face, v_face, depth_float, raw_west, raw_east, u_west, u_east, depth_west, depth_east))
    rhs = lax.optimization_barrier(jnp.sum(adj_tracer, axis=1))
    wet_top = wet_levels(depth_float, 1)[0]
    east_open = wet_top * jnp.concatenate([wet_top[..., 1:], wet_levels(depth_east[..., :1], 1)[0]], axis=-1)
    west_open = wet_top * jnp.concatenate([wet_levels(depth_west[..., 1:], 1)[0], wet_top[..., :-1]], axis=-1)
    north_open = wet_top * jnp.pad(wet_top[:, 1:, :], ((0, 0), (0, 1), (0, 0)))
    south_open = wet_top * jnp.pad(wet_top[:, :-1, :], ((0, 0), (1, 0), (0, 0)))

    def surface_operator(pressure_field):
        from_west, from_east = seam_neighbours(pressure_field, seam_flip, 1)
        east_vals = jnp.concatenate([pressure_field[..., 1:], from_east], axis=-1)
        west_vals = jnp.concatenate([from_west, pressure_field[..., :-1]], axis=-1)
        north_vals = jnp.pad(pressure_field[:, 1:, :], ((0, 0), (0, 1), (0, 0)))
        south_vals = jnp.pad(pressure_field[:, :-1, :], ((0, 0), (1, 0), (0, 0)))
        applied = surface_diag * pressure_field + east_open * (pressure_field - east_vals) + west_open * (pressure_field - west_vals)
        return applied + north_open * (pressure_field - north_vals) + south_open * (pressure_field - south_vals)
    solution = jnp.zeros_like(rhs)
    residual = rhs
    direction = rhs
    norm_now = jnp.sum(residual * residual)
    for iteration in range(ITERS):
        applied = surface_operator(direction)
        step_size = norm_now / jnp.sum(direction * applied)
        solution = solution + step_size * direction
        if iteration + 1 < ITERS:
            residual = residual - step_size * applied
            norm_next = jnp.sum(residual * residual)
            direction = residual + norm_next / norm_now * direction
            norm_now = norm_next
    return (adj_tracer, solution)
```

```python
import functools
import math

import jax
import jax.numpy as jnp
from jax import lax
from jax.experimental import pallas as pl
from jax.experimental.pallas import tpu as pltpu
from jax.sharding import PartitionSpec as P

MESH = pl.DeviceIdType.MESH

K = 6
ROWS = 32
COLS = 128
HALO = 8
EXT_ROWS = ROWS + 2 * HALO
EXT_COLS = 2 * COLS

TRACER, U, V, COT, DEPTH, DIAG = 0, K, 2 * K, 3 * K, 4 * K, 4 * K + 1
PLANES = 4 * K + 2
WIDTHS = [6] * K + [5] * K + [4] * K + [4] * K + [6, 1]
OFFSETS = [sum(WIDTHS[:i]) for i in range(PLANES)]

RELAX_MEAN, RELAX_SWING, DAY_STEPS = 0.5, 0.8, 24.0


def shift_x(value, by):
    return pltpu.roll(value, (-by) % value.shape[1], axis=1)


def shift_y(value, by):
    return pltpu.roll(value, (-by) % value.shape[0], axis=0)


def reversed_rows(block):
    row = lax.broadcasted_iota(jnp.int32, (8, block.shape[1]), 0)
    tiles = []
    for start in range(block.shape[0] - 8, -1, -8):
        tile = pltpu.roll(block[start : start + 8], 4, axis=0)
        tile = jnp.where(row % 4 < 2, pltpu.roll(tile, 6, axis=0), pltpu.roll(tile, 2, axis=0))
        tile = jnp.where(row % 2 < 1, pltpu.roll(tile, 7, axis=0), pltpu.roll(tile, 1, axis=0))
        tiles.append(tile)
    return jnp.concatenate(tiles, axis=0)


def groups(tile, col, sizes):
    size_x, size_z, size_y_lo = sizes
    x, z, y_lo = tile % size_x, (tile // size_x) % size_z, tile // (size_x * size_z)
    y, core = (col // 2) * size_y_lo + y_lo, col % 2
    size_y = 2 * size_y_lo

    def device(x, y, z, core):
        return (((y % size_y_lo) * size_z + z) * size_x + x, (y // size_y_lo) * 2 + core)

    chips = []
    for apart in range(1, 2 * size_x):
        place = (x * 2 + core + apart) % (2 * size_x)
        chips.append(device(place // 2, y, z, place % 2))
    alongs_y = [device(x, (y + apart) % size_y, z, core) for apart in range(1, size_y)]
    alongs_z = [device(x, y, (z + apart) % size_z, core) for apart in range(1, size_z)]
    return chips, alongs_y, alongs_z


def kernel(
    sizes,
    tracer_hbm,
    u_hbm,
    v_hbm,
    depth_hbm,
    cot_hbm,
    diag_hbm,
    flip_hbm,
    step_hbm,
    adj_hbm,
    pressure_hbm,
    ext,
    depth_int,
    flips,
    step,
    packed,
    plain,
    mirror,
    mixed,
    raw,
    adj,
    pressure,
    part0,
    part1,
    part2,
    sum0,
    sum1,
    sum2,
    load_sem,
    small_sem,
    store_sem,
    send_sem,
    recv_sem,
    part_send,
    part_recv,
):
    tiles = sizes[0] * sizes[1] * sizes[2]
    tile, col = lax.axis_index("tile"), lax.axis_index("col")
    east, west = (tile + 1) % tiles, (tile + tiles - 1) % tiles
    phases = groups(tile, col, sizes)

    barrier = pltpu.get_barrier_semaphore()
    peers = [(side, other) for side in (east, west) for other in range(4)]
    peers += [(tile, (col + 1) % 4), (tile, (col + 3) % 4)]
    for phase in phases:
        peers += phase
    for peer in peers:
        pl.semaphore_signal(barrier, inc=1, device_id=peer, device_id_type=MESH)

    inner = pl.ds(HALO, ROWS)
    loads = [
        pltpu.make_async_copy(src.at[0], ext.at[pl.ds(plane, K), inner, pl.ds(0, COLS)], load_sem.at[i])
        for i, (src, plane) in enumerate(((tracer_hbm, TRACER), (u_hbm, U), (v_hbm, V), (cot_hbm, COT)))
    ]
    loads.append(pltpu.make_async_copy(diag_hbm.at[0], ext.at[DIAG, inner, pl.ds(0, COLS)], load_sem.at[4]))
    loads.append(pltpu.make_async_copy(depth_hbm.at[0], depth_int, load_sem.at[5]))
    smalls = [
        pltpu.make_async_copy(flip_hbm, flips, small_sem.at[0]),
        pltpu.make_async_copy(step_hbm, step, small_sem.at[1]),
    ]
    for copy in loads + smalls:
        copy.start()
    for copy in loads:
        copy.wait()
    ext[DEPTH, HALO : HALO + ROWS, 0:COLS] = depth_int[...].astype(jnp.float32)

    lane = lax.broadcasted_iota(jnp.int32, (ROWS, COLS), 1)
    for side in range(2):
        block = jnp.zeros((ROWS, COLS), jnp.float32)
        for plane in range(PLANES):
            width, offset = WIDTHS[plane], OFFSETS[plane]
            own = ext[plane, HALO : HALO + ROWS, 0:COLS]
            moved = pltpu.roll(own, (offset + width if side == 0 else offset) % COLS, axis=1)
            block = jnp.where(lane >= offset, moved, block)
        packed[side] = block

    pl.semaphore_wait(barrier, len(peers))

    first, last, whole = pl.ds(0, HALO), pl.ds(ROWS - HALO, HALO), pl.ds(0, ROWS)
    below, above = pl.ds(0, HALO), pl.ds(HALO + ROWS, HALO)
    sends = []

    def seam_copy(side, kind, source, target_block, target, target_col):
        index = side * 6 + kind
        return pltpu.make_async_remote_copy(
            src_ref=packed.at[side, source],
            dst_ref=target_block.at[side, target],
            send_sem=send_sem.at[index],
            recv_sem=recv_sem.at[index],
            device_id=(east if side == 0 else west, target_col),
            device_id_type=MESH,
        )

    def row_copy(index, source, target, target_col):
        return pltpu.make_async_remote_copy(
            src_ref=ext.at[:, source, pl.ds(0, COLS)],
            dst_ref=ext.at[:, target, pl.ds(0, COLS)],
            send_sem=send_sem.at[index],
            recv_sem=recv_sem.at[index],
            device_id=(tile, target_col),
            device_id_type=MESH,
        )

    low, high = col > 0, col < 3
    sends.append((row_copy(12, pl.ds(ROWS, HALO), below, (col + 1) % 4), high, low))
    sends.append((row_copy(13, pl.ds(HALO, HALO), above, (col + 3) % 4), low, high))
    for side in range(2):
        sends.append((seam_copy(side, 3, whole, mirror, inner, 3 - col), None, None))
        sends.append((seam_copy(side, 4, last, mirror, below, (6 - col) % 4), high, high))
        sends.append((seam_copy(side, 5, first, mirror, above, (4 - col) % 4), low, low))
        sends.append((seam_copy(side, 0, whole, plain, inner, col), None, None))
        sends.append((seam_copy(side, 1, last, plain, below, (col + 1) % 4), high, low))
        sends.append((seam_copy(side, 2, first, plain, above, (col + 3) % 4), low, high))

    def maybe(condition, act):
        if condition is None:
            act()
        else:
            pl.when(condition)(act)

    for copy, sending, _ in sends:
        maybe(sending, copy.start)

    for copy in smalls:
        copy.wait()
    flip_east = flips[tile] == 1
    flip_west = flips[west] == 1
    angle = jnp.full((8, COLS), step[0], jnp.int32).astype(jnp.float32) * (2.0 * math.pi / DAY_STEPS)
    kept = 1.0 - (RELAX_MEAN * (1.0 + RELAX_SWING * jnp.cos(angle)))[0:1, 0:1]

    for copy, _, receiving in sends:
        maybe(receiving, copy.wait_recv)

    lane = lax.broadcasted_iota(jnp.int32, (EXT_ROWS, COLS), 1)
    speeds = (lane >= OFFSETS[V]) & (lane < OFFSETS[V + K])

    def beyond_seam(side, flip):
        turned = reversed_rows(mirror[side])
        turned = jnp.where(speeds, -shift_y(turned, 1), turned)
        return jnp.where(flip, turned, plain[side])

    from_west = beyond_seam(0, flip_west)
    from_east = beyond_seam(1, flip_east)
    for plane in range(PLANES):
        width, offset = WIDTHS[plane], OFFSETS[plane]
        right = pltpu.roll(from_east, (COLS - offset) % COLS, axis=1)
        left = pltpu.roll(from_west, (COLS - width - offset) % COLS, axis=1)
        if plane == DEPTH:
            beside = jnp.where(lane < width, right, jnp.where(lane >= COLS - width, left, 0.0))
        else:
            beside = jnp.where(lane < COLS // 2, right, left)
        ext[plane, :, COLS:EXT_COLS] = beside

    row = lax.broadcasted_iota(jnp.int32, (EXT_ROWS, EXT_COLS), 0) + (col * ROWS - HALO)
    inside = (row >= 0) & (row < 4 * ROWS)
    depth = jnp.where(inside, ext[DEPTH], 0.0)
    open_x = jnp.minimum(depth, shift_x(depth, 1))
    open_y = jnp.minimum(depth, shift_y(depth, 1))

    def gated(levels, level, value):
        return jnp.where(levels > float(level), value, 0.0)

    for k in range(K):
        masked = gated(depth, k, ext[TRACER + k])
        change = None
        for shift, levels, speed in ((shift_x, open_x, U), (shift_y, open_y, V)):
            front = shift(masked, 1)
            flux = ext[speed + k] * (
                (7.0 / 12.0) * (masked + front) - (1.0 / 12.0) * (shift(masked, -1) + shift(masked, 2))
            )
            flux = gated(levels, k, flux - 0.4 * (front - masked))
            flux = flux - shift(flux, -1)
            change = flux if change is None else change + flux
        mixed[k] = gated(depth, k, masked - 0.2 * change)

    carry = None
    for k in range(K):
        weight = gated(depth, k, ext[COT + k])
        total = weight * kept if k == 0 else weight
        if carry is not None:
            total = total + carry
        if k + 1 < K:
            gap = mixed[k + 1] - mixed[k]
            bend = jnp.tanh(2.0 * gap)
            slope = 0.6 + 0.5 * bend + gap * (1.0 - bend * bend)
            carry = 0.3 * (weight - gated(depth, k + 1, ext[COT + k + 1])) * gated(depth, k + 1, slope)
            total = total - carry
        raw[k] = gated(depth, k, total)

    rhs = None
    for k in range(K):
        weight = raw[k]
        total = weight
        for shift, levels, speed in ((shift_x, open_x, U), (shift_y, open_y, V)):
            scaled = gated(levels, k, 0.2 * (shift(weight, 1) - weight))
            carried = gated(levels, k, ext[speed + k] * (1.0 / 12.0)) * scaled
            seven, rest = 7.0 * carried, 0.4 * scaled
            total = total + (seven + rest - shift(carried, 1))
            total = total + shift(seven - rest - shift(carried, -1), -1)
        total = gated(depth, k, total)
        adj[k] = total[HALO : HALO + ROWS, 0:COLS]
        rhs = total if rhs is None else rhs + total
    store_adj = pltpu.make_async_copy(adj, adj_hbm.at[0], store_sem.at[0])
    store_adj.start()

    diagonal = jnp.where(inside, ext[DIAG], 0.0)

    def applied(field):
        across = gated(open_x, 0, field - shift_x(field, 1))
        along = gated(open_y, 0, field - shift_y(field, 1))
        return diagonal * field + (across - shift_x(across, -1)) + (along - shift_y(along, -1))

    once = applied(rhs)
    twice = applied(once)[HALO : HALO + ROWS, 0:COLS]
    once = once[HALO : HALO + ROWS, 0:COLS]
    rhs = rhs[HALO : HALO + ROWS, 0:COLS]
    lane = lax.broadcasted_iota(jnp.int32, (1, COLS), 1)
    partial = jnp.zeros((1, COLS), jnp.float32)
    for place, product in enumerate((rhs * rhs, rhs * once, once * once, rhs * twice, once * twice)):
        value = jnp.sum(jnp.sum(product, axis=0, keepdims=True), axis=1, keepdims=True)
        partial = jnp.where(lane == place, value, partial)

    begun = []
    for i, (phase, part, sums) in enumerate(zip(phases, (part0, part1, part2), (sum0, sum1, sum2))):
        part[...] = partial
        for slot, peer in enumerate(phase):
            copy = pltpu.make_async_remote_copy(
                src_ref=part,
                dst_ref=sums.at[slot],
                send_sem=part_send.at[i],
                recv_sem=part_recv.at[i],
                device_id=peer,
                device_id_type=MESH,
            )
            copy.start()
        begun.append(pltpu.make_async_copy(sums, sums, part_send.at[i]))
        pltpu.make_async_copy(sums, sums, part_recv.at[i]).wait()
        for slot in range(len(phase)):
            partial = partial + sums[slot]

    def scalar(place):
        return jnp.sum(jnp.where(lane == place, partial, 0.0), axis=1, keepdims=True)

    g00, g01, g11, g02, g12 = [scalar(place) for place in range(5)]
    step0 = g00 / g01
    norm1 = g00 - 2.0 * step0 * g01 + step0 * step0 * g11
    lift = 1.0 + norm1 / g00
    step1 = norm1 / (
        lift * (lift * g01 - step0 * g02) - step0 * (lift * g11 - step0 * g12)
    )
    pressure[...] = (step0 + step1 * lift) * rhs - (step1 * step0) * once
    store_pressure = pltpu.make_async_copy(pressure, pressure_hbm.at[0], store_sem.at[1])
    store_pressure.start()

    for copy, sending, _ in sends:
        maybe(sending, copy.wait_send)
    for copy in begun:
        copy.wait()
    store_adj.wait()
    store_pressure.wait()


def solution(mesh):
    sizes = (4, 12, 4)
    any_space = pl.BlockSpec(memory_space=pl.ANY)

    def step(tracer_old, u_face, v_face, depth_levels, cotangent, surface_diag, seam_flip, step_index):
        return pl.pallas_call(
            functools.partial(kernel, sizes),
            out_shape=(
                jax.ShapeDtypeStruct(tracer_old.shape, jnp.float32),
                jax.ShapeDtypeStruct(surface_diag.shape, jnp.float32),
            ),
            in_specs=[any_space] * 8,
            out_specs=(any_space, any_space),
            scratch_shapes=[
                pltpu.VMEM((PLANES, EXT_ROWS, EXT_COLS), jnp.float32),
                pltpu.VMEM((ROWS, COLS), jnp.int32),
                pltpu.SMEM(seam_flip.shape, jnp.int32),
                pltpu.SMEM(step_index.shape, jnp.int32),
                pltpu.VMEM((2, ROWS, COLS), jnp.float32),
                pltpu.VMEM((2, EXT_ROWS, COLS), jnp.float32),
                pltpu.VMEM((2, EXT_ROWS, COLS), jnp.float32),
                pltpu.VMEM((K, EXT_ROWS, EXT_COLS), jnp.float32),
                pltpu.VMEM((K, EXT_ROWS, EXT_COLS), jnp.float32),
                pltpu.VMEM((K, ROWS, COLS), jnp.float32),
                pltpu.VMEM((ROWS, COLS), jnp.float32),
                pltpu.VMEM((1, COLS), jnp.float32),
                pltpu.VMEM((1, COLS), jnp.float32),
                pltpu.VMEM((1, COLS), jnp.float32),
                pltpu.VMEM((7, 1, COLS), jnp.float32),
                pltpu.VMEM((7, 1, COLS), jnp.float32),
                pltpu.VMEM((11, 1, COLS), jnp.float32),
                pltpu.SemaphoreType.DMA((6,)),
                pltpu.SemaphoreType.DMA((2,)),
                pltpu.SemaphoreType.DMA((2,)),
                pltpu.SemaphoreType.DMA((14,)),
                pltpu.SemaphoreType.DMA((14,)),
                pltpu.SemaphoreType.DMA((3,)),
                pltpu.SemaphoreType.DMA((3,)),
            ],
            compiler_params=pltpu.CompilerParams(
                collective_id=0, has_side_effects=True, vmem_limit_bytes=32 << 20
            ),
        )(tracer_old, u_face, v_face, depth_levels, cotangent, surface_diag, seam_flip, step_index)

    in_specs = (
        P("tile", None, "col", None),
        P("tile", None, "col", None),
        P("tile", None, "col", None),
        P("tile", "col", None),
        P("tile", None, "col", None),
        P("tile", "col", None),
        P(),
        P(),
    )
    out_specs = (P("tile", None, "col", None), P("tile", "col", None))
    return jax.shard_map(step, mesh=mesh, in_specs=in_specs, out_specs=out_specs, check_vma=False)
```

```python
import functools
import math

import jax
import jax.numpy as jnp
from jax import lax
from jax.experimental import pallas as pl
from jax.experimental.pallas import tpu as pltpu
from jax.sharding import PartitionSpec as P

MESH = pl.DeviceIdType.MESH

K = 6
ROWS = 32
COLS = 128
HALO = 8
EXT_ROWS = ROWS + 2 * HALO
EXT_COLS = 2 * COLS

TRACER, U, V, COT, DEPTH, DIAG = 0, K, 2 * K, 3 * K, 4 * K, 4 * K + 1
PLANES = 4 * K + 2
WIDTHS = [6] * K + [5] * K + [4] * K + [4] * K + [6, 1]
OFFSETS = [sum(WIDTHS[:i]) for i in range(PLANES)]

RELAX_MEAN, RELAX_SWING, DAY_STEPS = 0.5, 0.8, 24.0


def shift_x(value, by):
    return pltpu.roll(value, (-by) % value.shape[1], axis=1)


def shift_y(value, by):
    return pltpu.roll(value, (-by) % value.shape[0], axis=0)


def reversed_rows(block):
    row = lax.broadcasted_iota(jnp.int32, (8, block.shape[1]), 0)
    tiles = []
    for start in range(block.shape[0] - 8, -1, -8):
        tile = pltpu.roll(block[start : start + 8], 4, axis=0)
        tile = jnp.where(row % 4 < 2, pltpu.roll(tile, 6, axis=0), pltpu.roll(tile, 2, axis=0))
        tile = jnp.where(row % 2 < 1, pltpu.roll(tile, 7, axis=0), pltpu.roll(tile, 1, axis=0))
        tiles.append(tile)
    return jnp.concatenate(tiles, axis=0)


def groups(tile, col, sizes):
    size_x, size_z, size_y_lo = sizes
    x, z = lax.rem(tile, size_x), lax.rem(lax.div(tile, size_x), size_z)
    y_lo = lax.div(tile, size_x * size_z)
    y_hi, core = lax.div(col, 2), lax.rem(col, 2)
    y = y_hi * size_y_lo + y_lo
    size_y = 2 * size_y_lo

    def device(x, y, z, core):
        y_hi = lax.div(y, size_y_lo)
        y_lo = y - y_hi * size_y_lo
        return ((y_lo * size_z + z) * size_x + x, y_hi * 2 + core)

    def farthest_first(count):
        return sorted(range(1, count), key=lambda apart: -min(apart, count - apart))

    columns = []
    for apart in farthest_first(2 * size_z):
        place = lax.rem(z * 2 + core + apart, 2 * size_z)
        columns.append(device(x, y, lax.div(place, 2), lax.rem(place, 2)))
    xs = [lax.rem(x + apart, size_x) for apart in range(size_x)]
    ys = [lax.rem(y + apart, size_y) for apart in range(size_y)]
    planes = []
    for apart in sorted(
        range(1, size_x * size_y),
        key=lambda a: -min(a % size_x, size_x - a % size_x) - min(a // size_x, size_y - a // size_x),
    ):
        planes.append(device(xs[apart % size_x], ys[apart // size_x], z, core))
    return columns, planes


def kernel(
    sizes,
    tracer_hbm,
    u_hbm,
    v_hbm,
    depth_hbm,
    cot_hbm,
    diag_hbm,
    flip_hbm,
    step_hbm,
    adj_out,
    pressure_out,
    ext,
    depth_int,
    flips,
    step,
    packed,
    rows_out,
    rows_in,
    plain,
    mirror,
    mixed,
    raw,
    part0,
    part1,
    sum0,
    sum1,
    load_sem,
    small_sem,
    send_sem,
    recv_sem,
    part_send,
    part_recv,
):
    tiles = sizes[0] * sizes[1] * sizes[2]
    tile, col = lax.axis_index("tile"), lax.axis_index("col")
    east, west = lax.rem(tile + 1, tiles), lax.rem(tile + tiles - 1, tiles)
    phases = groups(tile, col, sizes)

    barrier = pltpu.get_barrier_semaphore()
    peers = [(side, other) for side in (east, west) for other in range(4)]
    peers += [(tile, lax.rem(col + 1, 4)), (tile, lax.rem(col + 3, 4))]
    for phase in phases:
        peers += phase
    inner = pl.ds(HALO, ROWS)
    loads = [
        pltpu.make_async_copy(src.at[0], ext.at[pl.ds(plane, K), inner, pl.ds(0, COLS)], load_sem.at[i])
        for i, (src, plane) in enumerate(((tracer_hbm, TRACER), (u_hbm, U), (v_hbm, V), (cot_hbm, COT)))
    ]
    loads.append(pltpu.make_async_copy(diag_hbm.at[0], ext.at[DIAG, inner, pl.ds(0, COLS)], load_sem.at[4]))
    loads.append(pltpu.make_async_copy(depth_hbm.at[0], depth_int, load_sem.at[5]))
    smalls = [
        pltpu.make_async_copy(flip_hbm, flips, small_sem.at[0]),
        pltpu.make_async_copy(step_hbm, step, small_sem.at[1]),
    ]
    for copy in loads + smalls:
        copy.start()
    for peer in peers:
        pl.semaphore_signal(barrier, inc=1, device_id=peer, device_id_type=MESH)

    for copy in loads:
        copy.wait()
    ext[DEPTH, HALO : HALO + ROWS, 0:COLS] = depth_int[...].astype(jnp.float32)

    lane = lax.broadcasted_iota(jnp.int32, (ROWS, COLS), 1)
    for side in range(2):
        block = jnp.zeros((ROWS, COLS), jnp.float32)
        for plane in range(PLANES):
            width, offset = WIDTHS[plane], OFFSETS[plane]
            own = ext[plane, HALO : HALO + ROWS, 0:COLS]
            moved = pltpu.roll(own, (offset + width if side == 0 else offset) % COLS, axis=1)
            block = jnp.where(lane >= offset, moved, block)
        packed[side] = block

    spot = lax.broadcasted_iota(jnp.int32, (HALO, COLS), 0)

    def end_tile(plane, way):
        start = ROWS if way == 0 else HALO
        return ext[plane, start : start + HALO, 0:COLS]

    for way in range(2):
        half = (spot >= 4) if way == 0 else (spot < 4)
        six = (spot >= 2) if way == 0 else (spot < 6)
        for k in range(K):
            tracer_tile, v_tile = end_tile(TRACER + k, way), end_tile(V + k, way)
            if way == 0:
                tracer_tile = jnp.where(six, tracer_tile, pltpu.roll(v_tile, 6, axis=0))
            rows_out[way, k] = tracer_tile
            rows_out[way, K + k] = jnp.where(
                half, end_tile(U + k, way), pltpu.roll(end_tile(COT + k, way), 4, axis=0)
            )
            if k % 2 == 0:
                other = pltpu.roll(end_tile(V + k + 1, way), 4, axis=0)
                rows_out[way, 2 * K + k // 2] = jnp.where(half, v_tile, other)
        diagonal_tile = pltpu.roll(end_tile(DIAG, way), 1 if way == 0 else 7, axis=0)
        rows_out[way, 2 * K + K // 2] = jnp.where(six, end_tile(DEPTH, way), diagonal_tile)

    pl.semaphore_wait(barrier, len(peers))

    first, last, whole = pl.ds(0, HALO), pl.ds(ROWS - HALO, HALO), pl.ds(0, ROWS)
    below, above = pl.ds(0, HALO), pl.ds(HALO + ROWS, HALO)
    sends = []

    def seam_copy(side, kind, source, target_block, target, target_col):
        index = side * 6 + kind
        return pltpu.make_async_remote_copy(
            src_ref=packed.at[side, source],
            dst_ref=target_block.at[side, target],
            send_sem=send_sem.at[index],
            recv_sem=recv_sem.at[index],
            device_id=(east if side == 0 else west, target_col),
            device_id_type=MESH,
        )

    def row_copy(index, way, target_col):
        return pltpu.make_async_remote_copy(
            src_ref=rows_out.at[way],
            dst_ref=rows_in.at[way],
            send_sem=send_sem.at[index],
            recv_sem=recv_sem.at[index],
            device_id=(tile, target_col),
            device_id_type=MESH,
        )

    low, high = col > 0, col < 3
    for side in range(2):
        sends.append((seam_copy(side, 3, whole, mirror, inner, 3 - col), None, None))
        sends.append((seam_copy(side, 4, last, mirror, below, lax.rem(6 - col, 4)), high, high))
        sends.append((seam_copy(side, 5, first, mirror, above, lax.rem(4 - col, 4)), low, low))
        sends.append((seam_copy(side, 0, whole, plain, inner, col), None, None))
        sends.append((seam_copy(side, 1, last, plain, below, lax.rem(col + 1, 4)), high, low))
        sends.append((seam_copy(side, 2, first, plain, above, lax.rem(col + 3, 4)), low, high))
    sends.append((row_copy(12, 0, lax.rem(col + 1, 4)), high, low))
    sends.append((row_copy(13, 1, lax.rem(col + 3, 4)), low, high))

    def maybe(condition, act):
        if condition is None:
            act()
        else:
            pl.when(condition)(act)

    for copy, sending, _ in sends:
        maybe(sending, copy.start)

    for copy in smalls:
        copy.wait()
    flip_east = flips[tile] == 1
    flip_west = flips[west] == 1
    angle = jnp.full((8, COLS), step[0], jnp.int32).astype(jnp.float32) * (2.0 * math.pi / DAY_STEPS)
    kept = 1.0 - (RELAX_MEAN * (1.0 + RELAX_SWING * jnp.cos(angle)))[0:1, 0:1]

    for copy, _, receiving in sends:
        maybe(receiving, copy.wait_recv)

    for way in range(2):
        half = (spot >= 4) if way == 0 else (spot < 4)
        start = 0 if way == 0 else HALO + ROWS

        def put(plane, value):
            ext[plane, start : start + HALO, 0:COLS] = value

        for k in range(K):
            tracer_tile, mixed_tile = rows_in[way, k], rows_in[way, K + k]
            put(TRACER + k, tracer_tile)
            put(U + k, mixed_tile)
            put(COT + k, pltpu.roll(mixed_tile, 4, axis=0))
            v_tile = rows_in[way, 2 * K + k // 2]
            if k % 2 == 1:
                v_tile = pltpu.roll(v_tile, 4, axis=0)
            if way == 0:
                v_tile = jnp.where(half, v_tile, pltpu.roll(tracer_tile, 2, axis=0))
            put(V + k, v_tile)
        depth_tile = rows_in[way, 2 * K + K // 2]
        put(DEPTH, depth_tile)
        put(DIAG, pltpu.roll(depth_tile, 7 if way == 0 else 1, axis=0))

    lane = lax.broadcasted_iota(jnp.int32, (EXT_ROWS, COLS), 1)
    speeds = (lane >= OFFSETS[V]) & (lane < OFFSETS[V + K])

    def beyond_seam(side, flip):
        turned = reversed_rows(mirror[side])
        turned = jnp.where(speeds, -shift_y(turned, 1), turned)
        return jnp.where(flip, turned, plain[side])

    from_west = beyond_seam(0, flip_west)
    from_east = beyond_seam(1, flip_east)
    for plane in range(PLANES):
        width, offset = WIDTHS[plane], OFFSETS[plane]
        right = pltpu.roll(from_east, (COLS - offset) % COLS, axis=1)
        left = pltpu.roll(from_west, (COLS - width - offset) % COLS, axis=1)
        if plane == DEPTH:
            beside = jnp.where(lane < width, right, jnp.where(lane >= COLS - width, left, 0.0))
        else:
            beside = jnp.where(lane < COLS // 2, right, left)
        ext[plane, :, COLS:EXT_COLS] = beside

    row = lax.broadcasted_iota(jnp.int32, (EXT_ROWS, EXT_COLS), 0) + (col * ROWS - HALO)
    inside = (row >= 0) & (row < 4 * ROWS)
    place = row - col * ROWS
    depth = jnp.where(inside & (place >= -6) & (place < ROWS + 6), ext[DEPTH], 0.0)
    open_x = jnp.minimum(depth, shift_x(depth, 1))
    open_y = jnp.minimum(depth, shift_y(depth, 1))

    def gated(levels, level, value):
        return jnp.where(levels > float(level), value, 0.0)

    for k in range(K):
        masked = gated(depth, k, ext[TRACER + k])
        change = None
        for shift, levels, speed in ((shift_x, open_x, U), (shift_y, open_y, V)):
            front = shift(masked, 1)
            flux = ext[speed + k] * (
                (7.0 / 12.0) * (masked + front) - (1.0 / 12.0) * (shift(masked, -1) + shift(masked, 2))
            )
            flux = gated(levels, k, flux - 0.4 * (front - masked))
            flux = flux - shift(flux, -1)
            change = flux if change is None else change + flux
        mixed[k] = gated(depth, k, masked - 0.2 * change)

    carry = None
    for k in range(K):
        weight = gated(depth, k, ext[COT + k])
        total = weight * kept if k == 0 else weight
        if carry is not None:
            total = total + carry
        if k + 1 < K:
            gap = mixed[k + 1] - mixed[k]
            bend = jnp.tanh(2.0 * gap)
            slope = 0.6 + 0.5 * bend + gap * (1.0 - bend * bend)
            carry = 0.3 * (weight - gated(depth, k + 1, ext[COT + k + 1])) * gated(depth, k + 1, slope)
            total = total - carry
        raw[k] = gated(depth, k, total)

    rhs = None
    for k in range(K):
        weight = raw[k]
        total = weight
        for shift, levels, speed in ((shift_x, open_x, U), (shift_y, open_y, V)):
            scaled = gated(levels, k, 0.2 * (shift(weight, 1) - weight))
            carried = gated(levels, k, ext[speed + k] * (1.0 / 12.0)) * scaled
            seven, rest = 7.0 * carried, 0.4 * scaled
            total = total + (seven + rest - shift(carried, 1))
            total = total + shift(seven - rest - shift(carried, -1), -1)
        total = gated(depth, k, total)
        adj_out[0, k] = total[HALO : HALO + ROWS, 0:COLS]
        rhs = total if rhs is None else rhs + total

    diagonal = jnp.where(inside, ext[DIAG], 0.0)

    def applied(field):
        across = gated(open_x, 0, field - shift_x(field, 1))
        along = gated(open_y, 0, field - shift_y(field, 1))
        return diagonal * field + (across - shift_x(across, -1)) + (along - shift_y(along, -1))

    once = applied(rhs)
    twice = applied(once)[HALO : HALO + ROWS, 0:COLS]
    once = once[HALO : HALO + ROWS, 0:COLS]
    rhs = rhs[HALO : HALO + ROWS, 0:COLS]
    lane = lax.broadcasted_iota(jnp.int32, (1, COLS), 1)
    partial = jnp.zeros((1, COLS), jnp.float32)
    for place, product in enumerate((rhs * rhs, rhs * once, once * once, rhs * twice, once * twice)):
        value = jnp.sum(jnp.sum(product, axis=0, keepdims=True), axis=1, keepdims=True)
        partial = jnp.where(lane == place, value, partial)

    begun = []
    for i, (phase, part, sums) in enumerate(zip(phases, (part0, part1), (sum0, sum1))):
        part[...] = partial
        for slot, peer in enumerate(phase):
            copy = pltpu.make_async_remote_copy(
                src_ref=part,
                dst_ref=sums.at[slot],
                send_sem=part_send.at[i],
                recv_sem=part_recv.at[i],
                device_id=peer,
                device_id_type=MESH,
            )
            copy.start()
        begun.append(pltpu.make_async_copy(sums, sums, part_send.at[i]))
        pltpu.make_async_copy(sums, sums, part_recv.at[i]).wait()
        for slot in range(len(phase)):
            partial = partial + sums[slot]

    def scalar(place):
        return jnp.sum(jnp.where(lane == place, partial, 0.0), axis=1, keepdims=True)

    g00, g01, g11, g02, g12 = [scalar(place) for place in range(5)]
    step0 = g00 / g01
    norm1 = g00 - 2.0 * step0 * g01 + step0 * step0 * g11
    lift = 1.0 + norm1 / g00
    step1 = norm1 / (
        lift * (lift * g01 - step0 * g02) - step0 * (lift * g11 - step0 * g12)
    )
    pressure_out[0] = (step0 + step1 * lift) * rhs - (step1 * step0) * once

    for copy, sending, _ in sends:
        maybe(sending, copy.wait_send)
    for copy in begun:
        copy.wait()


def solution(mesh):
    sizes = (4, 12, 4)
    any_space = pl.BlockSpec(memory_space=pl.ANY)

    def step(tracer_old, u_face, v_face, depth_levels, cotangent, surface_diag, seam_flip, step_index):
        return pl.pallas_call(
            functools.partial(kernel, sizes),
            out_shape=(
                jax.ShapeDtypeStruct(tracer_old.shape, jnp.float32),
                jax.ShapeDtypeStruct(surface_diag.shape, jnp.float32),
            ),
            in_specs=[any_space] * 8,
            out_specs=(pl.BlockSpec(memory_space=pltpu.VMEM), pl.BlockSpec(memory_space=pltpu.VMEM)),
            scratch_shapes=[
                pltpu.VMEM((PLANES, EXT_ROWS, EXT_COLS), jnp.float32),
                pltpu.VMEM((ROWS, COLS), jnp.int32),
                pltpu.SMEM(seam_flip.shape, jnp.int32),
                pltpu.SMEM(step_index.shape, jnp.int32),
                pltpu.VMEM((2, ROWS, COLS), jnp.float32),
                pltpu.VMEM((2, 2 * K + K // 2 + 1, HALO, COLS), jnp.float32),
                pltpu.VMEM((2, 2 * K + K // 2 + 1, HALO, COLS), jnp.float32),
                pltpu.VMEM((2, EXT_ROWS, COLS), jnp.float32),
                pltpu.VMEM((2, EXT_ROWS, COLS), jnp.float32),
                pltpu.VMEM((K, EXT_ROWS, EXT_COLS), jnp.float32),
                pltpu.VMEM((K, EXT_ROWS, EXT_COLS), jnp.float32),
                pltpu.VMEM((1, COLS), jnp.float32),
                pltpu.VMEM((1, COLS), jnp.float32),
                pltpu.VMEM((23, 1, COLS), jnp.float32),
                pltpu.VMEM((31, 1, COLS), jnp.float32),
                pltpu.SemaphoreType.DMA((6,)),
                pltpu.SemaphoreType.DMA((2,)),
                pltpu.SemaphoreType.DMA((14,)),
                pltpu.SemaphoreType.DMA((14,)),
                pltpu.SemaphoreType.DMA((2,)),
                pltpu.SemaphoreType.DMA((2,)),
            ],
            compiler_params=pltpu.CompilerParams(
                collective_id=0, has_side_effects=True
            ),
        )(tracer_old, u_face, v_face, depth_levels, cotangent, surface_diag, seam_flip, step_index)

    in_specs = (
        P("tile", None, "col", None),
        P("tile", None, "col", None),
        P("tile", None, "col", None),
        P("tile", "col", None),
        P("tile", None, "col", None),
        P("tile", "col", None),
        P(),
        P(),
    )
    out_specs = (P("tile", None, "col", None), P("tile", "col", None))
    return jax.shard_map(step, mesh=mesh, in_specs=in_specs, out_specs=out_specs, check_vma=False)
```

```python
import functools
import math

import jax
import jax.numpy as jnp
from jax import lax
from jax.experimental import pallas as pl
from jax.experimental.pallas import tpu as pltpu
from jax.sharding import PartitionSpec as P

MESH = pl.DeviceIdType.MESH

K = 6
ROWS = 32
COLS = 128
HALO = 8
EXT_ROWS = ROWS + 2 * HALO
EXT_COLS = 2 * COLS

TRACER, U, V, COT, DEPTH, DIAG = 0, K, 2 * K, 3 * K, 4 * K, 4 * K + 1
PLANES = 4 * K + 2
WIDTHS = [6] * K + [5] * K + [4] * K + [4] * K + [6, 1]
OFFSETS = [sum(WIDTHS[:i]) for i in range(PLANES)]

RELAX_MEAN, RELAX_SWING, DAY_STEPS = 0.5, 0.8, 24.0


def shift_x(value, by):
    return pltpu.roll(value, (-by) % value.shape[1], axis=1)


def shift_y(value, by):
    return pltpu.roll(value, (-by) % value.shape[0], axis=0)


def reversed_rows(block):
    row = lax.broadcasted_iota(jnp.int32, (8, block.shape[1]), 0)
    tiles = []
    for start in range(block.shape[0] - 8, -1, -8):
        tile = pltpu.roll(block[start : start + 8], 4, axis=0)
        tile = jnp.where(row % 4 < 2, pltpu.roll(tile, 6, axis=0), pltpu.roll(tile, 2, axis=0))
        tile = jnp.where(row % 2 < 1, pltpu.roll(tile, 7, axis=0), pltpu.roll(tile, 1, axis=0))
        tiles.append(tile)
    return jnp.concatenate(tiles, axis=0)


def groups(tile, col, sizes):
    size_x, size_z, size_y_lo = sizes
    x, z = lax.rem(tile, size_x), lax.rem(lax.div(tile, size_x), size_z)
    y_lo = lax.div(tile, size_x * size_z)
    y_hi, core = lax.div(col, 2), lax.rem(col, 2)
    y = y_hi * size_y_lo + y_lo
    size_y = 2 * size_y_lo

    def device(x, y, z, core):
        y_hi = lax.div(y, size_y_lo)
        y_lo = y - y_hi * size_y_lo
        return ((y_lo * size_z + z) * size_x + x, y_hi * 2 + core)

    def farthest_first(count):
        return sorted(range(1, count), key=lambda apart: -min(apart, count - apart))

    columns = []
    for apart in farthest_first(2 * size_z):
        place = lax.rem(z * 2 + core + apart, 2 * size_z)
        columns.append(device(x, y, lax.div(place, 2), lax.rem(place, 2)))
    xs = [lax.rem(x + apart, size_x) for apart in range(size_x)]
    ys = [lax.rem(y + apart, size_y) for apart in range(size_y)]
    planes = []
    for apart in sorted(
        range(1, size_x * size_y),
        key=lambda a: -min(a % size_x, size_x - a % size_x) - min(a // size_x, size_y - a // size_x),
    ):
        planes.append(device(xs[apart % size_x], ys[apart // size_x], z, core))
    return columns, planes


def kernel(
    sizes,
    tracer_hbm,
    u_hbm,
    v_hbm,
    depth_hbm,
    cot_hbm,
    diag_hbm,
    flip_hbm,
    step_hbm,
    adj_hbm,
    pressure_hbm,
    ext,
    depth_int,
    flips,
    step,
    packed,
    rows_out,
    rows_in,
    adj_out,
    pressure_out,
    plain,
    mirror,
    mixed,
    raw,
    part0,
    part1,
    sum0,
    sum1,
    load_sem,
    small_sem,
    store_sem,
    send_sem,
    recv_sem,
    part_send,
    part_recv,
):
    tiles = sizes[0] * sizes[1] * sizes[2]
    tile, col = lax.axis_index("tile"), lax.axis_index("col")
    east, west = lax.rem(tile + 1, tiles), lax.rem(tile + tiles - 1, tiles)
    phases = groups(tile, col, sizes)

    barrier = pltpu.get_barrier_semaphore()
    peers = [(side, other) for side in (east, west) for other in range(4)]
    peers += [(tile, lax.rem(col + 1, 4)), (tile, lax.rem(col + 3, 4))]
    for phase in phases:
        peers += phase
    inner = pl.ds(HALO, ROWS)
    loads = [
        pltpu.make_async_copy(src.at[0], ext.at[pl.ds(plane, K), inner, pl.ds(0, COLS)], load_sem.at[i])
        for i, (src, plane) in enumerate(((tracer_hbm, TRACER), (u_hbm, U), (v_hbm, V), (cot_hbm, COT)))
    ]
    loads.append(pltpu.make_async_copy(diag_hbm.at[0], ext.at[DIAG, inner, pl.ds(0, COLS)], load_sem.at[4]))
    loads.append(pltpu.make_async_copy(depth_hbm.at[0], depth_int, load_sem.at[5]))
    smalls = [
        pltpu.make_async_copy(flip_hbm, flips, small_sem.at[0]),
        pltpu.make_async_copy(step_hbm, step, small_sem.at[1]),
    ]
    for copy in loads + smalls:
        copy.start()
    for peer in peers:
        pl.semaphore_signal(barrier, inc=1, device_id=peer, device_id_type=MESH)

    for copy in loads:
        copy.wait()
    ext[DEPTH, HALO : HALO + ROWS, 0:COLS] = depth_int[...].astype(jnp.float32)

    lane = lax.broadcasted_iota(jnp.int32, (ROWS, COLS), 1)
    for side in range(2):
        block = jnp.zeros((ROWS, COLS), jnp.float32)
        for plane in range(PLANES):
            width, offset = WIDTHS[plane], OFFSETS[plane]
            own = ext[plane, HALO : HALO + ROWS, 0:COLS]
            moved = pltpu.roll(own, (offset + width if side == 0 else offset) % COLS, axis=1)
            block = jnp.where(lane >= offset, moved, block)
        packed[side] = block

    spot = lax.broadcasted_iota(jnp.int32, (HALO, COLS), 0)

    def end_tile(plane, way):
        start = ROWS if way == 0 else HALO
        return ext[plane, start : start + HALO, 0:COLS]

    for way in range(2):
        half = (spot >= 4) if way == 0 else (spot < 4)
        six = (spot >= 2) if way == 0 else (spot < 6)
        for k in range(K):
            tracer_tile, v_tile = end_tile(TRACER + k, way), end_tile(V + k, way)
            if way == 0:
                tracer_tile = jnp.where(six, tracer_tile, pltpu.roll(v_tile, 6, axis=0))
            rows_out[way, k] = tracer_tile
            rows_out[way, K + k] = jnp.where(
                half, end_tile(U + k, way), pltpu.roll(end_tile(COT + k, way), 4, axis=0)
            )
            if k % 2 == 0:
                other = pltpu.roll(end_tile(V + k + 1, way), 4, axis=0)
                rows_out[way, 2 * K + k // 2] = jnp.where(half, v_tile, other)
        diagonal_tile = pltpu.roll(end_tile(DIAG, way), 1 if way == 0 else 7, axis=0)
        rows_out[way, 2 * K + K // 2] = jnp.where(six, end_tile(DEPTH, way), diagonal_tile)

    pl.semaphore_wait(barrier, len(peers))

    first, last, whole = pl.ds(0, HALO), pl.ds(ROWS - HALO, HALO), pl.ds(0, ROWS)
    below, above = pl.ds(0, HALO), pl.ds(HALO + ROWS, HALO)
    sends = []

    def seam_copy(side, kind, source, target_block, target, target_col):
        index = side * 6 + kind
        return pltpu.make_async_remote_copy(
            src_ref=packed.at[side, source],
            dst_ref=target_block.at[side, target],
            send_sem=send_sem.at[index],
            recv_sem=recv_sem.at[index],
            device_id=(east if side == 0 else west, target_col),
            device_id_type=MESH,
        )

    def row_copy(index, way, target_col):
        return pltpu.make_async_remote_copy(
            src_ref=rows_out.at[way],
            dst_ref=rows_in.at[way],
            send_sem=send_sem.at[index],
            recv_sem=recv_sem.at[index],
            device_id=(tile, target_col),
            device_id_type=MESH,
        )

    low, high = col > 0, col < 3
    for side in range(2):
        sends.append((seam_copy(side, 3, whole, mirror, inner, 3 - col), None, None))
        sends.append((seam_copy(side, 4, last, mirror, below, lax.rem(6 - col, 4)), high, high))
        sends.append((seam_copy(side, 5, first, mirror, above, lax.rem(4 - col, 4)), low, low))
        sends.append((seam_copy(side, 0, whole, plain, inner, col), None, None))
        sends.append((seam_copy(side, 1, last, plain, below, lax.rem(col + 1, 4)), high, low))
        sends.append((seam_copy(side, 2, first, plain, above, lax.rem(col + 3, 4)), low, high))
    sends.append((row_copy(12, 0, lax.rem(col + 1, 4)), high, low))
    sends.append((row_copy(13, 1, lax.rem(col + 3, 4)), low, high))

    def maybe(condition, act):
        if condition is None:
            act()
        else:
            pl.when(condition)(act)

    for copy, sending, _ in sends:
        maybe(sending, copy.start)

    for copy in smalls:
        copy.wait()
    flip_east = flips[tile] == 1
    flip_west = flips[west] == 1
    angle = jnp.full((8, COLS), step[0], jnp.int32).astype(jnp.float32) * (2.0 * math.pi / DAY_STEPS)
    kept = 1.0 - (RELAX_MEAN * (1.0 + RELAX_SWING * jnp.cos(angle)))[0:1, 0:1]

    for copy, _, receiving in sends:
        maybe(receiving, copy.wait_recv)

    for way in range(2):
        half = (spot >= 4) if way == 0 else (spot < 4)
        start = 0 if way == 0 else HALO + ROWS

        def put(plane, value):
            ext[plane, start : start + HALO, 0:COLS] = value

        for k in range(K):
            tracer_tile, mixed_tile = rows_in[way, k], rows_in[way, K + k]
            put(TRACER + k, tracer_tile)
            put(U + k, mixed_tile)
            put(COT + k, pltpu.roll(mixed_tile, 4, axis=0))
            v_tile = rows_in[way, 2 * K + k // 2]
            if k % 2 == 1:
                v_tile = pltpu.roll(v_tile, 4, axis=0)
            if way == 0:
                v_tile = jnp.where(half, v_tile, pltpu.roll(tracer_tile, 2, axis=0))
            put(V + k, v_tile)
        depth_tile = rows_in[way, 2 * K + K // 2]
        put(DEPTH, depth_tile)
        put(DIAG, pltpu.roll(depth_tile, 7 if way == 0 else 1, axis=0))

    lane = lax.broadcasted_iota(jnp.int32, (EXT_ROWS, COLS), 1)
    speeds = (lane >= OFFSETS[V]) & (lane < OFFSETS[V + K])

    def beyond_seam(side, flip):
        turned = reversed_rows(mirror[side])
        turned = jnp.where(speeds, -shift_y(turned, 1), turned)
        return jnp.where(flip, turned, plain[side])

    from_west = beyond_seam(0, flip_west)
    from_east = beyond_seam(1, flip_east)
    for plane in range(PLANES):
        width, offset = WIDTHS[plane], OFFSETS[plane]
        right = pltpu.roll(from_east, (COLS - offset) % COLS, axis=1)
        left = pltpu.roll(from_west, (COLS - width - offset) % COLS, axis=1)
        if plane == DEPTH:
            beside = jnp.where(lane < width, right, jnp.where(lane >= COLS - width, left, 0.0))
        else:
            beside = jnp.where(lane < COLS // 2, right, left)
        ext[plane, :, COLS:EXT_COLS] = beside

    row = lax.broadcasted_iota(jnp.int32, (EXT_ROWS, EXT_COLS), 0) + (col * ROWS - HALO)
    inside = (row >= 0) & (row < 4 * ROWS)
    place = row - col * ROWS
    depth = jnp.where(inside & (place >= -6) & (place < ROWS + 6), ext[DEPTH], 0.0)
    open_x = jnp.minimum(depth, shift_x(depth, 1))
    open_y = jnp.minimum(depth, shift_y(depth, 1))

    def gated(levels, level, value):
        return jnp.where(levels > float(level), value, 0.0)

    for k in range(K):
        masked = gated(depth, k, ext[TRACER + k])
        change = None
        for shift, levels, speed in ((shift_x, open_x, U), (shift_y, open_y, V)):
            front = shift(masked, 1)
            flux = ext[speed + k] * (
                (7.0 / 12.0) * (masked + front) - (1.0 / 12.0) * (shift(masked, -1) + shift(masked, 2))
            )
            flux = gated(levels, k, flux - 0.4 * (front - masked))
            flux = flux - shift(flux, -1)
            change = flux if change is None else change + flux
        mixed[k] = gated(depth, k, masked - 0.2 * change)

    carry = None
    for k in range(K):
        weight = gated(depth, k, ext[COT + k])
        total = weight * kept if k == 0 else weight
        if carry is not None:
            total = total + carry
        if k + 1 < K:
            gap = mixed[k + 1] - mixed[k]
            bend = jnp.tanh(2.0 * gap)
            slope = 0.6 + 0.5 * bend + gap * (1.0 - bend * bend)
            carry = 0.3 * (weight - gated(depth, k + 1, ext[COT + k + 1])) * gated(depth, k + 1, slope)
            total = total - carry
        raw[k] = gated(depth, k, total)

    rhs = None
    for k in range(K):
        weight = raw[k]
        total = weight
        for shift, levels, speed in ((shift_x, open_x, U), (shift_y, open_y, V)):
            scaled = gated(levels, k, 0.2 * (shift(weight, 1) - weight))
            carried = gated(levels, k, ext[speed + k] * (1.0 / 12.0)) * scaled
            seven, rest = 7.0 * carried, 0.4 * scaled
            total = total + (seven + rest - shift(carried, 1))
            total = total + shift(seven - rest - shift(carried, -1), -1)
        total = gated(depth, k, total)
        adj_out[k] = total[HALO : HALO + ROWS, 0:COLS]
        rhs = total if rhs is None else rhs + total

    store_adj = pltpu.make_async_copy(adj_out, adj_hbm.at[0], store_sem.at[0])
    store_adj.start()

    diagonal = jnp.where(inside, ext[DIAG], 0.0)

    def applied(field):
        across = gated(open_x, 0, field - shift_x(field, 1))
        along = gated(open_y, 0, field - shift_y(field, 1))
        return diagonal * field + (across - shift_x(across, -1)) + (along - shift_y(along, -1))

    once = applied(rhs)
    twice = applied(once)[HALO : HALO + ROWS, 0:COLS]
    once = once[HALO : HALO + ROWS, 0:COLS]
    rhs = rhs[HALO : HALO + ROWS, 0:COLS]
    lane = lax.broadcasted_iota(jnp.int32, (1, COLS), 1)
    partial = jnp.zeros((1, COLS), jnp.float32)
    for place, product in enumerate((rhs * rhs, rhs * once, once * once, rhs * twice, once * twice)):
        value = jnp.sum(jnp.sum(product, axis=0, keepdims=True), axis=1, keepdims=True)
        partial = jnp.where(lane == place, value, partial)

    begun = []
    for i, (phase, part, sums) in enumerate(zip(phases, (part0, part1), (sum0, sum1))):
        part[...] = partial
        for slot, peer in enumerate(phase):
            copy = pltpu.make_async_remote_copy(
                src_ref=part,
                dst_ref=sums.at[slot],
                send_sem=part_send.at[i],
                recv_sem=part_recv.at[i],
                device_id=peer,
                device_id_type=MESH,
            )
            copy.start()
        begun.append(pltpu.make_async_copy(sums, sums, part_send.at[i]))
        pltpu.make_async_copy(sums, sums, part_recv.at[i]).wait()
        for slot in range(len(phase)):
            partial = partial + sums[slot]

    def scalar(place):
        return jnp.sum(jnp.where(lane == place, partial, 0.0), axis=1, keepdims=True)

    g00, g01, g11, g02, g12 = [scalar(place) for place in range(5)]
    step0 = g00 / g01
    norm1 = g00 - 2.0 * step0 * g01 + step0 * step0 * g11
    lift = 1.0 + norm1 / g00
    step1 = norm1 / (
        lift * (lift * g01 - step0 * g02) - step0 * (lift * g11 - step0 * g12)
    )
    pressure_out[...] = (step0 + step1 * lift) * rhs - (step1 * step0) * once

    store_pressure = pltpu.make_async_copy(pressure_out, pressure_hbm.at[0], store_sem.at[1])
    store_pressure.start()
    for copy, sending, _ in sends:
        maybe(sending, copy.wait_send)
    for copy in begun:
        copy.wait()
    store_adj.wait()
    store_pressure.wait()


def hand_over(adj_in, pressure_in, adj_out, pressure_out, adj_held, pressure_held, sem):
    parts = [(pressure_in, pressure_held, pressure_out)]
    parts += [(adj_in.at[:, h], adj_held.at[:, h], adj_out.at[:, h]) for h in (pl.ds(0, K // 2), pl.ds(K // 2, K // 2))]
    loads = [pltpu.make_async_copy(a, b, sem.at[0, i]) for i, (a, b, _) in enumerate(parts)]
    stores = [pltpu.make_async_copy(b, c, sem.at[1, i]) for i, (_, b, c) in enumerate(parts)]
    for copy in loads:
        copy.start()
    for load, store in zip(loads, stores):
        load.wait()
        store.start()
    for copy in stores:
        copy.wait()


def solution(mesh):
    sizes = (4, 12, 4)
    any_space = pl.BlockSpec(memory_space=pl.ANY)

    def step(tracer_old, u_face, v_face, depth_levels, cotangent, surface_diag, seam_flip, step_index):
        results = pl.pallas_call(
            functools.partial(kernel, sizes),
            out_shape=(
                jax.ShapeDtypeStruct(tracer_old.shape, jnp.float32),
                jax.ShapeDtypeStruct(surface_diag.shape, jnp.float32),
            ),
            in_specs=[any_space] * 8,
            out_specs=(any_space, any_space),
            scratch_shapes=[
                pltpu.VMEM((PLANES, EXT_ROWS, EXT_COLS), jnp.float32),
                pltpu.VMEM((ROWS, COLS), jnp.int32),
                pltpu.SMEM(seam_flip.shape, jnp.int32),
                pltpu.SMEM(step_index.shape, jnp.int32),
                pltpu.VMEM((2, ROWS, COLS), jnp.float32),
                pltpu.VMEM((2, 2 * K + K // 2 + 1, HALO, COLS), jnp.float32),
                pltpu.VMEM((2, 2 * K + K // 2 + 1, HALO, COLS), jnp.float32),
                pltpu.VMEM((K, ROWS, COLS), jnp.float32),
                pltpu.VMEM((ROWS, COLS), jnp.float32),
                pltpu.VMEM((2, EXT_ROWS, COLS), jnp.float32),
                pltpu.VMEM((2, EXT_ROWS, COLS), jnp.float32),
                pltpu.VMEM((K, EXT_ROWS, EXT_COLS), jnp.float32),
                pltpu.VMEM((K, EXT_ROWS, EXT_COLS), jnp.float32),
                pltpu.VMEM((1, COLS), jnp.float32),
                pltpu.VMEM((1, COLS), jnp.float32),
                pltpu.VMEM((23, 1, COLS), jnp.float32),
                pltpu.VMEM((31, 1, COLS), jnp.float32),
                pltpu.SemaphoreType.DMA((6,)),
                pltpu.SemaphoreType.DMA((2,)),
                pltpu.SemaphoreType.DMA((2,)),
                pltpu.SemaphoreType.DMA((14,)),
                pltpu.SemaphoreType.DMA((14,)),
                pltpu.SemaphoreType.DMA((2,)),
                pltpu.SemaphoreType.DMA((2,)),
            ],
            compiler_params=pltpu.CompilerParams(
                collective_id=0, has_side_effects=True
            ),
        )(tracer_old, u_face, v_face, depth_levels, cotangent, surface_diag, seam_flip, step_index)

        return pl.pallas_call(
            hand_over,
            out_shape=(
                jax.ShapeDtypeStruct(tracer_old.shape, jnp.float32),
                jax.ShapeDtypeStruct(surface_diag.shape, jnp.float32),
            ),
            in_specs=[any_space] * 2,
            out_specs=(any_space, any_space),
            scratch_shapes=[
                pltpu.VMEM((1, K, ROWS, COLS), jnp.float32),
                pltpu.VMEM((1, ROWS, COLS), jnp.float32),
                pltpu.SemaphoreType.DMA((2, 3)),
            ],
        )(*results)

    in_specs = (
        P("tile", None, "col", None),
        P("tile", None, "col", None),
        P("tile", None, "col", None),
        P("tile", "col", None),
        P("tile", None, "col", None),
        P("tile", "col", None),
        P(),
        P(),
    )
    out_specs = (P("tile", None, "col", None), P("tile", "col", None))
    return jax.shard_map(step, mesh=mesh, in_specs=in_specs, out_specs=out_specs, check_vma=False)
```

```python
import functools
import math

import jax
import jax.numpy as jnp
from jax import lax
from jax.experimental import pallas as pl
from jax.experimental.pallas import tpu as pltpu
from jax.sharding import PartitionSpec as P

MESH = pl.DeviceIdType.MESH

K = 6
ROWS = 32
COLS = 128
HALO = 8
EXT_ROWS = ROWS + 2 * HALO
EXT_COLS = 2 * COLS

TRACER, U, V, COT, DEPTH, DIAG = 0, K, 2 * K, 3 * K, 4 * K, 4 * K + 1
PLANES = 4 * K + 2
WIDTHS = [6] * K + [5] * K + [4] * K + [4] * K + [6, 1]
OFFSETS = [sum(WIDTHS[:i]) for i in range(PLANES)]

RELAX_MEAN, RELAX_SWING, DAY_STEPS = 0.5, 0.8, 24.0


def shift_x(value, by):
    return pltpu.roll(value, (-by) % value.shape[1], axis=1)


def shift_y(value, by):
    return pltpu.roll(value, (-by) % value.shape[0], axis=0)


def reversed_rows(block):
    row = lax.broadcasted_iota(jnp.int32, (8, block.shape[1]), 0)
    tiles = []
    for start in range(block.shape[0] - 8, -1, -8):
        tile = pltpu.roll(block[start : start + 8], 4, axis=0)
        tile = jnp.where(row % 4 < 2, pltpu.roll(tile, 6, axis=0), pltpu.roll(tile, 2, axis=0))
        tile = jnp.where(row % 2 < 1, pltpu.roll(tile, 7, axis=0), pltpu.roll(tile, 1, axis=0))
        tiles.append(tile)
    return jnp.concatenate(tiles, axis=0)


def groups(tile, col, sizes):
    size_x, size_z, size_y_lo = sizes
    x, z = lax.rem(tile, size_x), lax.rem(lax.div(tile, size_x), size_z)
    y_lo = lax.div(tile, size_x * size_z)
    y_hi, core = lax.div(col, 2), lax.rem(col, 2)
    y = y_hi * size_y_lo + y_lo
    size_y = 2 * size_y_lo

    def device(x, y, z, core):
        y_hi = lax.div(y, size_y_lo)
        y_lo = y - y_hi * size_y_lo
        return ((y_lo * size_z + z) * size_x + x, y_hi * 2 + core)

    def farthest_first(count):
        return sorted(range(1, count), key=lambda apart: -min(apart, count - apart))

    columns = []
    for apart in farthest_first(2 * size_z):
        place = lax.rem(z * 2 + core + apart, 2 * size_z)
        columns.append(device(x, y, lax.div(place, 2), lax.rem(place, 2)))
    xs = [lax.rem(x + apart, size_x) for apart in range(size_x)]
    ys = [lax.rem(y + apart, size_y) for apart in range(size_y)]
    planes = []
    for apart in sorted(
        range(1, size_x * size_y),
        key=lambda a: -min(a % size_x, size_x - a % size_x) - min(a // size_x, size_y - a // size_x),
    ):
        planes.append(device(xs[apart % size_x], ys[apart // size_x], z, core))
    return columns, planes


def kernel(
    sizes,
    tracer_hbm,
    u_hbm,
    v_hbm,
    depth_hbm,
    cot_hbm,
    diag_hbm,
    flip_hbm,
    step_hbm,
    adj_hbm,
    pressure_hbm,
    ext,
    depth_int,
    flips,
    step,
    packed,
    rows_out,
    rows_in,
    adj_out,
    pressure_out,
    plain,
    mirror,
    mixed,
    raw,
    part0,
    part1,
    sum0,
    sum1,
    load_sem,
    small_sem,
    store_sem,
    send_sem,
    recv_sem,
    part_send,
    part_recv,
):
    tiles = sizes[0] * sizes[1] * sizes[2]
    tile, col = lax.axis_index("tile"), lax.axis_index("col")
    east, west = lax.rem(tile + 1, tiles), lax.rem(tile + tiles - 1, tiles)
    phases = groups(tile, col, sizes)

    barrier = pltpu.get_barrier_semaphore()
    peers = [(side, other) for side in (east, west) for other in range(4)]
    peers += [(tile, lax.rem(col + 1, 4)), (tile, lax.rem(col + 3, 4))]
    for phase in phases:
        peers += phase
    inner = pl.ds(HALO, ROWS)
    loads = [
        pltpu.make_async_copy(src.at[0], ext.at[pl.ds(plane, K), inner, pl.ds(0, COLS)], load_sem.at[i])
        for i, (src, plane) in enumerate(((tracer_hbm, TRACER), (u_hbm, U), (v_hbm, V), (cot_hbm, COT)))
    ]
    loads.append(pltpu.make_async_copy(diag_hbm.at[0], ext.at[DIAG, inner, pl.ds(0, COLS)], load_sem.at[4]))
    loads.append(pltpu.make_async_copy(depth_hbm.at[0], depth_int, load_sem.at[5]))
    smalls = [
        pltpu.make_async_copy(flip_hbm, flips, small_sem.at[0]),
        pltpu.make_async_copy(step_hbm, step, small_sem.at[1]),
    ]
    for copy in loads + smalls:
        copy.start()
    for peer in peers:
        pl.semaphore_signal(barrier, inc=1, device_id=peer, device_id_type=MESH)

    for copy in loads:
        copy.wait()
    ext[DEPTH, HALO : HALO + ROWS, 0:COLS] = depth_int[...].astype(jnp.float32)

    lane = lax.broadcasted_iota(jnp.int32, (ROWS, COLS), 1)
    for side in range(2):
        block = jnp.zeros((ROWS, COLS), jnp.float32)
        for plane in range(PLANES):
            width, offset = WIDTHS[plane], OFFSETS[plane]
            own = ext[plane, HALO : HALO + ROWS, 0:COLS]
            moved = pltpu.roll(own, (offset + width if side == 0 else offset) % COLS, axis=1)
            block = jnp.where(lane >= offset, moved, block)
        packed[side] = block

    spot = lax.broadcasted_iota(jnp.int32, (HALO, COLS), 0)

    def end_tile(plane, way):
        start = ROWS if way == 0 else HALO
        return ext[plane, start : start + HALO, 0:COLS]

    for way in range(2):
        half = (spot >= 4) if way == 0 else (spot < 4)
        six = (spot >= 2) if way == 0 else (spot < 6)
        for k in range(K):
            tracer_tile, v_tile = end_tile(TRACER + k, way), end_tile(V + k, way)
            if way == 0:
                tracer_tile = jnp.where(six, tracer_tile, pltpu.roll(v_tile, 6, axis=0))
            rows_out[way, k] = tracer_tile
            rows_out[way, K + k] = jnp.where(
                half, end_tile(U + k, way), pltpu.roll(end_tile(COT + k, way), 4, axis=0)
            )
            if k % 2 == 0:
                other = pltpu.roll(end_tile(V + k + 1, way), 4, axis=0)
                rows_out[way, 2 * K + k // 2] = jnp.where(half, v_tile, other)
        diagonal_tile = pltpu.roll(end_tile(DIAG, way), 1 if way == 0 else 7, axis=0)
        rows_out[way, 2 * K + K // 2] = jnp.where(six, end_tile(DEPTH, way), diagonal_tile)

    pl.semaphore_wait(barrier, len(peers))

    first, last, whole = pl.ds(0, HALO), pl.ds(ROWS - HALO, HALO), pl.ds(0, ROWS)
    below, above = pl.ds(0, HALO), pl.ds(HALO + ROWS, HALO)
    sends = []

    def seam_copy(side, kind, source, target_block, target, target_col):
        index = side * 6 + kind
        return pltpu.make_async_remote_copy(
            src_ref=packed.at[side, source],
            dst_ref=target_block.at[side, target],
            send_sem=send_sem.at[index],
            recv_sem=recv_sem.at[index],
            device_id=(east if side == 0 else west, target_col),
            device_id_type=MESH,
        )

    def row_copy(index, way, target_col):
        return pltpu.make_async_remote_copy(
            src_ref=rows_out.at[way],
            dst_ref=rows_in.at[way],
            send_sem=send_sem.at[index],
            recv_sem=recv_sem.at[index],
            device_id=(tile, target_col),
            device_id_type=MESH,
        )

    low, high = col > 0, col < 3
    for side in range(2):
        sends.append((seam_copy(side, 3, whole, mirror, inner, 3 - col), None, None))
        sends.append((seam_copy(side, 4, last, mirror, below, lax.rem(6 - col, 4)), high, high))
        sends.append((seam_copy(side, 5, first, mirror, above, lax.rem(4 - col, 4)), low, low))
        sends.append((seam_copy(side, 0, whole, plain, inner, col), None, None))
        sends.append((seam_copy(side, 1, last, plain, below, lax.rem(col + 1, 4)), high, low))
        sends.append((seam_copy(side, 2, first, plain, above, lax.rem(col + 3, 4)), low, high))
    sends.append((row_copy(12, 0, lax.rem(col + 1, 4)), high, low))
    sends.append((row_copy(13, 1, lax.rem(col + 3, 4)), low, high))

    def maybe(condition, act):
        if condition is None:
            act()
        else:
            pl.when(condition)(act)

    for copy, sending, _ in sends:
        maybe(sending, copy.start)

    for copy in smalls:
        copy.wait()
    flip_east = flips[tile] == 1
    flip_west = flips[west] == 1
    angle = jnp.full((8, COLS), step[0], jnp.int32).astype(jnp.float32) * (2.0 * math.pi / DAY_STEPS)
    kept = 1.0 - (RELAX_MEAN * (1.0 + RELAX_SWING * jnp.cos(angle)))[0:1, 0:1]

    seams, ends = sends[:-2], sends[-2:]
    for copy, _, receiving in seams:
        maybe(receiving, copy.wait_recv)


    lane = lax.broadcasted_iota(jnp.int32, (EXT_ROWS, COLS), 1)
    speeds = (lane >= OFFSETS[V]) & (lane < OFFSETS[V + K])

    def beyond_seam(side, flip):
        turned = reversed_rows(mirror[side])
        turned = jnp.where(speeds, -shift_y(turned, 1), turned)
        return jnp.where(flip, turned, plain[side])

    from_west = beyond_seam(0, flip_west)
    from_east = beyond_seam(1, flip_east)
    for plane in range(PLANES):
        width, offset = WIDTHS[plane], OFFSETS[plane]
        right = pltpu.roll(from_east, (COLS - offset) % COLS, axis=1)
        left = pltpu.roll(from_west, (COLS - width - offset) % COLS, axis=1)
        if plane == DEPTH:
            beside = jnp.where(lane < width, right, jnp.where(lane >= COLS - width, left, 0.0))
        else:
            beside = jnp.where(lane < COLS // 2, right, left)
        ext[plane, :, COLS:EXT_COLS] = beside

    for copy, _, receiving in ends:
        maybe(receiving, copy.wait_recv)
    for way in range(2):
        half = (spot >= 4) if way == 0 else (spot < 4)
        start = 0 if way == 0 else HALO + ROWS

        def put(plane, value):
            ext[plane, start : start + HALO, 0:COLS] = value

        for k in range(K):
            tracer_tile, mixed_tile = rows_in[way, k], rows_in[way, K + k]
            put(TRACER + k, tracer_tile)
            put(U + k, mixed_tile)
            put(COT + k, pltpu.roll(mixed_tile, 4, axis=0))
            v_tile = rows_in[way, 2 * K + k // 2]
            if k % 2 == 1:
                v_tile = pltpu.roll(v_tile, 4, axis=0)
            if way == 0:
                v_tile = jnp.where(half, v_tile, pltpu.roll(tracer_tile, 2, axis=0))
            put(V + k, v_tile)
        depth_tile = rows_in[way, 2 * K + K // 2]
        put(DEPTH, depth_tile)
        put(DIAG, pltpu.roll(depth_tile, 7 if way == 0 else 1, axis=0))

    row = lax.broadcasted_iota(jnp.int32, (EXT_ROWS, EXT_COLS), 0) + (col * ROWS - HALO)
    inside = (row >= 0) & (row < 4 * ROWS)
    place = row - col * ROWS
    depth = jnp.where(inside & (place >= -6) & (place < ROWS + 6), ext[DEPTH], 0.0)
    open_x = jnp.minimum(depth, shift_x(depth, 1))
    open_y = jnp.minimum(depth, shift_y(depth, 1))

    def gated(levels, level, value):
        return jnp.where(levels > float(level), value, 0.0)

    for k in range(K):
        masked = gated(depth, k, ext[TRACER + k])
        change = None
        for shift, levels, speed in ((shift_x, open_x, U), (shift_y, open_y, V)):
            front = shift(masked, 1)
            flux = ext[speed + k] * (
                (7.0 / 12.0) * (masked + front) - (1.0 / 12.0) * (shift(masked, -1) + shift(masked, 2))
            )
            flux = gated(levels, k, flux - 0.4 * (front - masked))
            flux = flux - shift(flux, -1)
            change = flux if change is None else change + flux
        mixed[k] = gated(depth, k, masked - 0.2 * change)

    carry = None
    for k in range(K):
        weight = gated(depth, k, ext[COT + k])
        total = weight * kept if k == 0 else weight
        if carry is not None:
            total = total + carry
        if k + 1 < K:
            gap = mixed[k + 1] - mixed[k]
            bend = jnp.tanh(2.0 * gap)
            slope = 0.6 + 0.5 * bend + gap * (1.0 - bend * bend)
            carry = 0.3 * (weight - gated(depth, k + 1, ext[COT + k + 1])) * gated(depth, k + 1, slope)
            total = total - carry
        raw[k] = gated(depth, k, total)

    rhs = None
    for k in range(K):
        weight = raw[k]
        total = weight
        for shift, levels, speed in ((shift_x, open_x, U), (shift_y, open_y, V)):
            scaled = gated(levels, k, 0.2 * (shift(weight, 1) - weight))
            carried = gated(levels, k, ext[speed + k] * (1.0 / 12.0)) * scaled
            seven, rest = 7.0 * carried, 0.4 * scaled
            total = total + (seven + rest - shift(carried, 1))
            total = total + shift(seven - rest - shift(carried, -1), -1)
        total = gated(depth, k, total)
        adj_out[k] = total[HALO : HALO + ROWS, 0:COLS]
        rhs = total if rhs is None else rhs + total

    store_adj = pltpu.make_async_copy(adj_out, adj_hbm.at[0], store_sem.at[0])
    store_adj.start()

    diagonal = jnp.where(inside, ext[DIAG], 0.0)

    def applied(field):
        across = gated(open_x, 0, field - shift_x(field, 1))
        along = gated(open_y, 0, field - shift_y(field, 1))
        return diagonal * field + (across - shift_x(across, -1)) + (along - shift_y(along, -1))

    once = applied(rhs)
    twice = applied(once)[HALO : HALO + ROWS, 0:COLS]
    once = once[HALO : HALO + ROWS, 0:COLS]
    rhs = rhs[HALO : HALO + ROWS, 0:COLS]
    lane = lax.broadcasted_iota(jnp.int32, (1, COLS), 1)
    partial = jnp.zeros((1, COLS), jnp.float32)
    for place, product in enumerate((rhs * rhs, rhs * once, once * once, rhs * twice, once * twice)):
        value = jnp.sum(jnp.sum(product, axis=0, keepdims=True), axis=1, keepdims=True)
        partial = jnp.where(lane == place, value, partial)

    begun = []
    for i, (phase, part, sums) in enumerate(zip(phases, (part0, part1), (sum0, sum1))):
        part[...] = partial
        for slot, peer in enumerate(phase):
            copy = pltpu.make_async_remote_copy(
                src_ref=part,
                dst_ref=sums.at[slot],
                send_sem=part_send.at[i],
                recv_sem=part_recv.at[i],
                device_id=peer,
                device_id_type=MESH,
            )
            copy.start()
        begun.append(pltpu.make_async_copy(sums, sums, part_send.at[i]))
        pltpu.make_async_copy(sums, sums, part_recv.at[i]).wait()
        for slot in range(len(phase)):
            partial = partial + sums[slot]

    def scalar(place):
        return jnp.sum(jnp.where(lane == place, partial, 0.0), axis=1, keepdims=True)

    g00, g01, g11, g02, g12 = [scalar(place) for place in range(5)]
    step0 = g00 / g01
    norm1 = g00 - 2.0 * step0 * g01 + step0 * step0 * g11
    lift = 1.0 + norm1 / g00
    step1 = norm1 / (
        lift * (lift * g01 - step0 * g02) - step0 * (lift * g11 - step0 * g12)
    )
    pressure_out[...] = (step0 + step1 * lift) * rhs - (step1 * step0) * once

    store_pressure = pltpu.make_async_copy(pressure_out, pressure_hbm.at[0], store_sem.at[1])
    store_pressure.start()
    for copy, sending, _ in sends:
        maybe(sending, copy.wait_send)
    for copy in begun:
        copy.wait()
    store_adj.wait()
    store_pressure.wait()


def hand_over(adj_in, pressure_in, adj_out, pressure_out, adj_held, pressure_held, sem):
    parts = [(pressure_in, pressure_held, pressure_out)]
    parts += [(adj_in.at[:, h], adj_held.at[:, h], adj_out.at[:, h]) for h in (pl.ds(0, K // 2), pl.ds(K // 2, K // 2))]
    loads = [pltpu.make_async_copy(a, b, sem.at[0, i]) for i, (a, b, _) in enumerate(parts)]
    stores = [pltpu.make_async_copy(b, c, sem.at[1, i]) for i, (_, b, c) in enumerate(parts)]
    for copy in loads:
        copy.start()
    for load, store in zip(loads, stores):
        load.wait()
        store.start()
    for copy in stores:
        copy.wait()


def solution(mesh):
    sizes = (4, 12, 4)
    any_space = pl.BlockSpec(memory_space=pl.ANY)

    def step(tracer_old, u_face, v_face, depth_levels, cotangent, surface_diag, seam_flip, step_index):
        results = pl.pallas_call(
            functools.partial(kernel, sizes),
            out_shape=(
                jax.ShapeDtypeStruct(tracer_old.shape, jnp.float32),
                jax.ShapeDtypeStruct(surface_diag.shape, jnp.float32),
            ),
            in_specs=[any_space] * 8,
            out_specs=(any_space, any_space),
            scratch_shapes=[
                pltpu.VMEM((PLANES, EXT_ROWS, EXT_COLS), jnp.float32),
                pltpu.VMEM((ROWS, COLS), jnp.int32),
                pltpu.SMEM(seam_flip.shape, jnp.int32),
                pltpu.SMEM(step_index.shape, jnp.int32),
                pltpu.VMEM((2, ROWS, COLS), jnp.float32),
                pltpu.VMEM((2, 2 * K + K // 2 + 1, HALO, COLS), jnp.float32),
                pltpu.VMEM((2, 2 * K + K // 2 + 1, HALO, COLS), jnp.float32),
                pltpu.VMEM((K, ROWS, COLS), jnp.float32),
                pltpu.VMEM((ROWS, COLS), jnp.float32),
                pltpu.VMEM((2, EXT_ROWS, COLS), jnp.float32),
                pltpu.VMEM((2, EXT_ROWS, COLS), jnp.float32),
                pltpu.VMEM((K, EXT_ROWS, EXT_COLS), jnp.float32),
                pltpu.VMEM((K, EXT_ROWS, EXT_COLS), jnp.float32),
                pltpu.VMEM((1, COLS), jnp.float32),
                pltpu.VMEM((1, COLS), jnp.float32),
                pltpu.VMEM((23, 1, COLS), jnp.float32),
                pltpu.VMEM((31, 1, COLS), jnp.float32),
                pltpu.SemaphoreType.DMA((6,)),
                pltpu.SemaphoreType.DMA((2,)),
                pltpu.SemaphoreType.DMA((2,)),
                pltpu.SemaphoreType.DMA((14,)),
                pltpu.SemaphoreType.DMA((14,)),
                pltpu.SemaphoreType.DMA((2,)),
                pltpu.SemaphoreType.DMA((2,)),
            ],
            compiler_params=pltpu.CompilerParams(
                collective_id=0, has_side_effects=True
            ),
        )(tracer_old, u_face, v_face, depth_levels, cotangent, surface_diag, seam_flip, step_index)

        return pl.pallas_call(
            hand_over,
            out_shape=(
                jax.ShapeDtypeStruct(tracer_old.shape, jnp.float32),
                jax.ShapeDtypeStruct(surface_diag.shape, jnp.float32),
            ),
            in_specs=[any_space] * 2,
            out_specs=(any_space, any_space),
            scratch_shapes=[
                pltpu.VMEM((1, K, ROWS, COLS), jnp.float32),
                pltpu.VMEM((1, ROWS, COLS), jnp.float32),
                pltpu.SemaphoreType.DMA((2, 3)),
            ],
        )(*results)

    in_specs = (
        P("tile", None, "col", None),
        P("tile", None, "col", None),
        P("tile", None, "col", None),
        P("tile", "col", None),
        P("tile", None, "col", None),
        P("tile", "col", None),
        P(),
        P(),
    )
    out_specs = (P("tile", None, "col", None), P("tile", "col", None))
    return jax.shard_map(step, mesh=mesh, in_specs=in_specs, out_specs=out_specs, check_vma=False)
```
